32 devices in a mesh: groups: 2 (over x), ctx: 16 (over z, y, core).
Axes of the slice: x: 2, y: 2, z: 4, core: 2. Of those that a mesh axis runs over, the one named last changes fastest.
Arguments:
- query_rows: bfloat16 [8192, 1024], P(('groups', 'ctx')), parts along dimension 0, may hold values from -6 to 6
- key_rows: bfloat16 [8192, 1024], P(('groups', 'ctx')), parts along dimension 0, may hold values from -6 to 6
- value_rows: bfloat16 [8192, 1024], P(('groups', 'ctx')), parts along dimension 0, may hold values from -6 to 6
- out_grad: bfloat16 [8192, 1024], P(('groups', 'ctx')), parts along dimension 0, may hold values from -6 to 6
Outputs:
- attended: bfloat16 [8192, 1024], P(('groups', 'ctx')), parts along dimension 0
- query_grad: bfloat16 [8192, 1024], P(('groups', 'ctx')), parts along dimension 0
- key_grad: bfloat16 [8192, 1024], P(('groups', 'ctx')), parts along dimension 0
- value_grad: bfloat16 [8192, 1024], P(('groups', 'ctx')), parts along dimension 0
The draws below stay inside these ranges and needn't reach their ends.
There are 2 independent parts, one for each index of `groups`. The reference program is written for one: setup_inputs(seed, part) draws one part's arguments, and reference() takes and returns one part's arrays. A program takes and returns all parts, laid end to end along the dimension named above; each array names one. Nothing has to cross between parts.
All inputs are finite; a program needn't handle non-finite values.
Results may differ from the reference program's by a relative error of at most 0.0059.
Values sent between devices are 32-bit elements; how exact they have to be, the bound alone decides.
A program may use at most 320 MiB of HBM per device.

```python
import jax
import jax.numpy as jnp
from jax import lax

HEADS = 8
DH = 128
TOK_DEV = 256
LENGTH = 4096
N_CTX = 16


def block_levels(rng, extent, shards, low, largest):
    def one(position, parts):
        heights = jax.random.uniform(jax.random.fold_in(jax.random.fold_in(rng, 6), position), (parts,), jnp.float32, low / len(shards), largest / len(shards))
        return jnp.repeat(jnp.exp(heights), extent[position] // parts).reshape((-1,) + (1,) * (len(extent) - position - 1))

    level = one(*shards[0])
    for cut in shards[1:]:
        level = level * one(*cut)
    return level


def normal_values(rng, extent, deviation, reach, split=(), kind=jnp.bfloat16):
    result = deviation * jax.random.normal(rng, extent, jnp.float32)
    if split:
        result = result * block_levels(rng, extent, split, -0.22, 0.18)
    return jnp.clip(result, -reach, reach).astype(kind)


def setup_inputs(seed: int = 0, part: int = 0) -> dict:
    streams_of = jax.random.split(jax.random.key(seed), 5)
    part_splits = jax.random.split(jax.random.fold_in(streams_of[4], part), 5)
    return {
        "query_rows": normal_values(part_splits[0], (LENGTH, HEADS * DH), 1.0, 6.0, ((0, 16),)),
        "key_rows": normal_values(part_splits[1], (LENGTH, HEADS * DH), 1.0, 6.0, ((0, 16),)),
        "value_rows": normal_values(part_splits[2], (LENGTH, HEADS * DH), 1.0, 6.0, ((0, 16),)),
        "out_grad": normal_values(part_splits[3], (LENGTH, HEADS * DH), 1.0, 6.0, ((0, 16),)),
    }


def block_terms(query_block, key_block, value_block, grad_block, prefix_low, suffix_low, scale_block):
    causal_mask = jnp.tril(jnp.ones((TOK_DEV, TOK_DEV), dtype=bool))
    qf = query_block.astype(jnp.float32)
    kf = key_block.astype(jnp.float32)
    vf = value_block.astype(jnp.float32)
    gf = grad_block.astype(jnp.float32)
    scores = jnp.einsum('thd,shd->hts', qf, kf)
    scores = jnp.where(causal_mask[None], scores, 0.0).astype(jnp.bfloat16).astype(jnp.float32)
    dscores = jnp.einsum('the,she->hts', gf, vf)
    dscores = jnp.where(causal_mask[None], dscores, 0.0).astype(jnp.bfloat16).astype(jnp.float32)
    prefix_f = prefix_low.astype(jnp.float32)
    suffix_f = suffix_low.astype(jnp.float32)
    attended = scale_block * (jnp.einsum('hts,she->the', scores, vf) + jnp.einsum('thd,hde->the', qf, prefix_f))
    query_grad = jnp.einsum('hts,shd->thd', dscores, kf) + jnp.einsum('the,hde->thd', gf, prefix_f)
    key_grad = jnp.einsum('hts,thd->shd', dscores, qf) + jnp.einsum('she,hde->shd', vf, suffix_f)
    value_grad = jnp.einsum('hts,the->she', scores, gf) + jnp.einsum('shd,hde->she', kf, suffix_f)
    return tuple((x.astype(jnp.bfloat16).reshape(TOK_DEV, HEADS * DH) for x in (attended, query_grad, key_grad, value_grad)))

def reference(query_rows, key_rows, value_rows, out_grad):
    shape4 = (N_CTX, TOK_DEV, HEADS, DH)
    queries = query_rows.reshape(shape4)
    key_blocks = key_rows.reshape(shape4)
    value_blocks = value_rows.reshape(shape4)
    positions = jnp.arange(LENGTH).astype(jnp.float32)
    row_scale = (1.0 / jnp.sqrt(DH * (positions + 1.0))).reshape(N_CTX, TOK_DEV, 1, 1).astype(jnp.float32)
    scaled_grad = (row_scale * out_grad.reshape(shape4).astype(jnp.float32)).astype(jnp.bfloat16)

    def forward_step(running, pieces):
        key_block, value_block = pieces
        state = jnp.einsum('thd,the->hde', key_block.astype(jnp.float32), value_block.astype(jnp.float32))
        return (running + state, running)

    def backward_step(running, pieces):
        query_block, grad_block = pieces
        state = jnp.einsum('thd,the->hde', query_block.astype(jnp.float32), grad_block.astype(jnp.float32))
        return (running + state, running)
    zero_state = jnp.zeros((HEADS, DH, DH), jnp.float32)
    _, prefixes = lax.scan(forward_step, zero_state, (key_blocks, value_blocks))
    _, suffixes = lax.scan(backward_step, zero_state, (queries, scaled_grad), reverse=True)
    prefixes = prefixes.astype(jnp.bfloat16)
    suffixes = suffixes.astype(jnp.bfloat16)

    def one_block(pieces):
        return block_terms(*pieces)
    results = lax.map(one_block, (queries, key_blocks, value_blocks, scaled_grad, prefixes, suffixes, row_scale))
    return tuple((x.reshape(LENGTH, HEADS * DH) for x in results))
```

```python
import functools

import jax
import jax.numpy as jnp
from jax import lax
from jax.experimental import pallas as pl
from jax.experimental.pallas import tpu as pltpu
from jax.sharding import PartitionSpec as P

DH = 128
MESH = pl.DeviceIdType.MESH
F32 = jnp.float32
BF16 = jnp.bfloat16


def dot(a, b, ca, cb):
    return lax.dot_general(a, b, (((ca,), (cb,)), ((), ())), preferred_element_type=F32)


def kernel(
    planes,
    heads,
    q_hbm,
    k_hbm,
    v_hbm,
    do_hbm,
    att_ref,
    qg_ref,
    kg_ref,
    vg_ref,
    q_ref,
    k_ref,
    v_ref,
    do_ref,
    g_ref,
    state,
    sib_in,
    y_out,
    y_in,
    z_out,
    z_in,
    ret_out,
    total,
    acc_a,
    acc_q,
    acc_k,
    acc_v,
    load_sem,
    sib_s,
    sib_r,
    y_s,
    y_r,
    z_s,
    z_r,
    ret_s,
    ret_r,
):
    tokens = q_ref.shape[0]
    group = lax.axis_index("groups")
    me = lax.axis_index("ctx")
    core = lax.rem(me, 2)
    row = lax.rem(me // 2, 2)
    plane = me // 4
    other = 1 - core
    step = 4 * (1 - 2 * core)
    has_prev = jnp.where(core == 0, plane > 0, plane < planes - 1)
    has_next = jnp.where(core == 0, plane < planes - 1, plane > 0)
    sibling = me + 1 - 2 * core
    partner = me + 2 - 4 * row
    is_low = row == core
    low = jnp.where(is_low, 1.0, 0.0).astype(F32)
    high = 1.0 - low

    def cols(h):
        return pl.ds(h * DH, DH)

    barrier = pltpu.get_barrier_semaphore()
    for device in (sibling, partner):
        pl.semaphore_signal(barrier, inc=1, device_id=(group, device), device_id_type=MESH)

    @pl.when(has_prev)
    def _():
        pl.semaphore_signal(barrier, inc=1, device_id=(group, me - step), device_id_type=MESH)

    @pl.when(has_next)
    def _():
        pl.semaphore_signal(barrier, inc=1, device_id=(group, me + step), device_id_type=MESH)

    first = heads // 2
    order = [h for i in range(first) for h in (i, first + i)]
    if heads % 2:
        order.append(heads - 1)

    loads = {}
    for h in order:
        for i, (src, dst) in enumerate(
            ((q_hbm, q_ref), (k_hbm, k_ref), (v_hbm, v_ref), (do_hbm, do_ref))
        ):
            loads[h, i] = pltpu.make_async_copy(
                src.at[:, cols(h)], dst.at[:, cols(h)], load_sem.at[i, h]
            )
            loads[h, i].start()

    @pl.when(jnp.logical_not(has_prev))
    def _():
        z_in[...] = jnp.zeros_like(z_in)

    def remote(src, dst, send, recv, device):
        return pltpu.make_async_remote_copy(
            src_ref=src,
            dst_ref=dst,
            send_sem=send,
            recv_sem=recv,
            device_id=(group, device),
            device_id_type=MESH,
        )

    def sib_copy(h):
        return remote(state.at[other, h], sib_in.at[h], sib_s.at[h], sib_r.at[h], sibling)

    def y_copy(h):
        return remote(y_out.at[h], y_in.at[h], y_s.at[h], y_r.at[h], partner)

    def z_copy(h):
        return remote(z_out.at[h], z_in.at[h], z_s.at[h], z_r.at[h], me + step)

    def ret_copy(h):
        return remote(ret_out.at[h], total.at[core, h], ret_s.at[h], ret_r.at[h], sibling)

    position = (me * tokens + lax.broadcasted_iota(jnp.int32, (tokens, DH), 0)).astype(F32)
    scale = 1.0 / jnp.sqrt(DH * (position + 1.0))

    for n, h in enumerate(order):
        for i in range(4):
            loads[h, i].wait()
        g = (scale * do_ref[:, cols(h)].astype(F32)).astype(BF16)
        g_ref[:, cols(h)] = g
        state[0, h] = dot(k_ref[:, cols(h)], v_ref[:, cols(h)], 0, 0)
        state[1, h] = dot(q_ref[:, cols(h)], g, 0, 0)
        if n == 0:
            pl.semaphore_wait(
                barrier, 2 + has_prev.astype(jnp.int32) + has_next.astype(jnp.int32)
            )
        sib_copy(h).start()

    def local(h):
        c = cols(h)
        q, k, v, g = q_ref[:, c], k_ref[:, c], v_ref[:, c], g_ref[:, c]
        t = lax.broadcasted_iota(jnp.int32, (tokens, tokens), 0)
        s = lax.broadcasted_iota(jnp.int32, (tokens, tokens), 1)
        scores = jnp.where(t >= s, dot(q, k, 1, 1), 0.0).astype(BF16)
        dscores = jnp.where(t >= s, dot(g, v, 1, 1), 0.0).astype(BF16)
        acc_a[:, c] = dot(scores, v, 1, 0)
        acc_q[:, c] = dot(dscores, k, 1, 0)
        acc_k[:, c] = dot(dscores, q, 0, 0)
        acc_v[:, c] = dot(scores, g, 0, 0)

    for h in order:
        sib_copy(h).wait_recv()
        if h < first:
            y_out[h] = state[core, h] + sib_in[h]
            y_copy(h).start()

    def give(h, base):
        total[core, h] = base
        ret_out[h] = base + state[core, h]
        ret_copy(h).start()

    def wait_plane(h):
        @pl.when(has_prev)
        def _():
            z_copy(h).wait_recv()

    def send_plane(h):
        @pl.when(has_next)
        def _():
            z_copy(h).start()

    for h in range(first, heads):
        wait_plane(h)
        here = state[core, h] + sib_in[h]
        z_out[h] = z_in[h] + here
        send_plane(h)
        y_out[h] = z_in[h] + low * here
        y_copy(h).start()
        local(h)

    for h in range(first):
        y_copy(h).wait_recv()
        wait_plane(h)
        before = z_in[h]
        z_out[h] = before + (y_out[h] + y_in[h])
        send_plane(h)
        give(h, before + high * y_in[h])
        local(h)

    for h in range(first, heads):
        y_copy(h).wait_recv()
        give(h, z_in[h] + y_in[h])

    for h in range(heads):
        ret_copy(h).wait_recv()
        c = cols(h)
        q, k, v, g = q_ref[:, c], k_ref[:, c], v_ref[:, c], g_ref[:, c]
        prefix = total[0, h].astype(BF16)
        suffix = total[1, h].astype(BF16)
        att_ref[:, c] = (scale * (acc_a[:, c] + dot(q, prefix, 1, 0))).astype(BF16)
        qg_ref[:, c] = (acc_q[:, c] + dot(g, prefix, 1, 1)).astype(BF16)
        kg_ref[:, c] = (acc_k[:, c] + dot(v, suffix, 1, 1)).astype(BF16)
        vg_ref[:, c] = (acc_v[:, c] + dot(k, suffix, 1, 0)).astype(BF16)

    for h in range(heads):
        sib_copy(h).wait_send()
        y_copy(h).wait_send()
        ret_copy(h).wait_send()

        @pl.when(has_next)
        def _():
            z_copy(h).wait_send()


def body(planes, query_rows, key_rows, value_rows, out_grad):
    tokens, width = query_rows.shape
    heads = width // DH
    out = jax.ShapeDtypeStruct((tokens, width), BF16)
    mat = pltpu.VMEM((heads, DH, DH), F32)
    mat2 = pltpu.VMEM((2, heads, DH, DH), F32)
    rows16 = pltpu.VMEM((tokens, width), BF16)
    rows32 = pltpu.VMEM((tokens, width), F32)
    sem = pltpu.SemaphoreType.DMA((heads,))
    return pl.pallas_call(
        functools.partial(kernel, planes, heads),
        out_shape=[out] * 4,
        in_specs=[pl.BlockSpec(memory_space=pl.ANY)] * 4,
        out_specs=[pl.BlockSpec(memory_space=pltpu.VMEM)] * 4,
        scratch_shapes=[rows16] * 5
        + [mat2, mat, mat, mat, mat, mat, mat, mat2]
        + [rows32] * 4
        + [pltpu.SemaphoreType.DMA((4, heads))]
        + [sem] * 8,
        compiler_params=pltpu.CompilerParams(
            collective_id=0, has_side_effects=True, vmem_limit_bytes=40 * 1024 * 1024
        ),
        cost_estimate=pl.CostEstimate(
            flops=18 * tokens * tokens * width, bytes_accessed=16 * tokens * width, transcendentals=0
        ),
    )(query_rows, key_rows, value_rows, out_grad)


def solution(mesh):
    spec = P(("groups", "ctx"), None)
    return jax.shard_map(
        functools.partial(body, mesh.shape["ctx"] // 4),
        mesh=mesh,
        in_specs=(spec,) * 4,
        out_specs=(spec,) * 4,
        check_vma=False,
    )
```

```python
import functools

import jax
import jax.numpy as jnp
from jax import lax
from jax.experimental import pallas as pl
from jax.experimental.pallas import tpu as pltpu
from jax.sharding import PartitionSpec as P

DH = 128
MESH = pl.DeviceIdType.MESH
F32 = jnp.float32
BF16 = jnp.bfloat16


def dot(a, b, ca, cb):
    return lax.dot_general(a, b, (((ca,), (cb,)), ((), ())), preferred_element_type=F32)


def kernel(
    planes,
    heads,
    q_hbm,
    k_hbm,
    v_hbm,
    do_hbm,
    att_ref,
    qg_ref,
    kg_ref,
    vg_ref,
    q_ref,
    k_ref,
    v_ref,
    do_ref,
    g_ref,
    state,
    sib_in,
    y_out,
    y_in,
    z_out,
    z_in,
    ret_out,
    total,
    acc_a,
    acc_q,
    acc_k,
    acc_v,
    load_sem,
    sib_s,
    sib_r,
    y_s,
    y_r,
    z_s,
    z_r,
    ret_s,
    ret_r,
):
    tokens = q_ref.shape[0]
    group = lax.axis_index("groups")
    me = lax.axis_index("ctx")
    core = lax.rem(me, 2)
    row = lax.rem(me // 2, 2)
    plane = me // 4
    other = 1 - core
    step = 4 * (1 - 2 * core)
    has_prev = jnp.where(core == 0, plane > 0, plane < planes - 1)
    has_next = jnp.where(core == 0, plane < planes - 1, plane > 0)
    sibling = me + 1 - 2 * core
    partner = me + 2 - 4 * row
    is_low = row == core
    low = jnp.where(is_low, 1.0, 0.0).astype(F32)
    high = 1.0 - low

    def cols(h):
        return pl.ds(h * DH, DH)

    barrier = pltpu.get_barrier_semaphore()
    for device in (sibling, partner):
        pl.semaphore_signal(barrier, inc=1, device_id=(group, device), device_id_type=MESH)

    @pl.when(has_prev)
    def _():
        pl.semaphore_signal(barrier, inc=1, device_id=(group, me - step), device_id_type=MESH)

    @pl.when(has_next)
    def _():
        pl.semaphore_signal(barrier, inc=1, device_id=(group, me + step), device_id_type=MESH)

    first = heads // 2
    order = [h for i in range(first) for h in (i, first + i)]
    if heads % 2:
        order.append(heads - 1)

    loads = {}
    for h in order:
        for i, (src, dst) in enumerate(
            ((q_hbm, q_ref), (k_hbm, k_ref), (v_hbm, v_ref), (do_hbm, do_ref))
        ):
            loads[h, i] = pltpu.make_async_copy(
                src.at[:, cols(h)], dst.at[:, cols(h)], load_sem.at[i, h]
            )
            loads[h, i].start()

    @pl.when(jnp.logical_not(has_prev))
    def _():
        z_in[...] = jnp.zeros_like(z_in)

    def remote(src, dst, send, recv, device):
        return pltpu.make_async_remote_copy(
            src_ref=src,
            dst_ref=dst,
            send_sem=send,
            recv_sem=recv,
            device_id=(group, device),
            device_id_type=MESH,
        )

    def sib_copy(h):
        return remote(state.at[other, h], sib_in.at[h], sib_s.at[h], sib_r.at[h], sibling)

    def y_copy(h):
        return remote(y_out.at[h], y_in.at[h], y_s.at[h], y_r.at[h], partner)

    def z_copy(h):
        return remote(z_out.at[h], z_in.at[h], z_s.at[h], z_r.at[h], me + step)

    def ret_copy(h):
        return remote(ret_out.at[h], total.at[core, h], ret_s.at[h], ret_r.at[h], sibling)

    position = (me * tokens + lax.broadcasted_iota(jnp.int32, (tokens, DH), 0)).astype(F32)
    scale = 1.0 / jnp.sqrt(DH * (position + 1.0))

    for n, h in enumerate(order):
        for i in range(4):
            loads[h, i].wait()
        g = (scale * do_ref[:, cols(h)].astype(F32)).astype(BF16)
        g_ref[:, cols(h)] = g
        state[0, h] = dot(k_ref[:, cols(h)], v_ref[:, cols(h)], 0, 0)
        state[1, h] = dot(q_ref[:, cols(h)], g, 0, 0)
        if n == 0:
            pl.semaphore_wait(
                barrier, 2 + has_prev.astype(jnp.int32) + has_next.astype(jnp.int32)
            )
        sib_copy(h).start()

    def local(h):
        c = cols(h)
        q, k, v, g = q_ref[:, c], k_ref[:, c], v_ref[:, c], g_ref[:, c]
        t = lax.broadcasted_iota(jnp.int32, (tokens, tokens), 0)
        s = lax.broadcasted_iota(jnp.int32, (tokens, tokens), 1)
        scores = jnp.where(t >= s, dot(q, k, 1, 1), 0.0).astype(BF16)
        dscores = jnp.where(t >= s, dot(g, v, 1, 1), 0.0).astype(BF16)
        acc_a[:, c] = dot(scores, v, 1, 0)
        acc_q[:, c] = dot(dscores, k, 1, 0)
        acc_k[:, c] = dot(dscores, q, 0, 0)
        acc_v[:, c] = dot(scores, g, 0, 0)

    for h in order:
        sib_copy(h).wait_recv()
        if h < first:
            y_out[h] = state[core, h] + sib_in[h]
            y_copy(h).start()

    def give(h, base):
        total[core, h] = base
        ret_out[h] = base + state[core, h]
        ret_copy(h).start()

    def wait_plane(h):
        @pl.when(has_prev)
        def _():
            z_copy(h).wait_recv()

    def send_plane(h):
        @pl.when(has_next)
        def _():
            z_copy(h).start()

    for h in range(first, heads):
        wait_plane(h)
        here = state[core, h] + sib_in[h]
        z_out[h] = z_in[h] + here
        send_plane(h)
        y_out[h] = z_in[h] + low * here
        y_copy(h).start()
        local(h)

    for h in range(first):
        y_copy(h).wait_recv()
        wait_plane(h)
        before = z_in[h]
        z_out[h] = before + (y_out[h] + y_in[h])
        send_plane(h)
        give(h, before + high * y_in[h])
        local(h)

    def finish(h):
        ret_copy(h).wait_recv()
        c = cols(h)
        q, k, v, g = q_ref[:, c], k_ref[:, c], v_ref[:, c], g_ref[:, c]
        prefix = total[0, h].astype(BF16)
        suffix = total[1, h].astype(BF16)
        att_ref[:, c] = (scale * (acc_a[:, c] + dot(q, prefix, 1, 0))).astype(BF16)
        qg_ref[:, c] = (acc_q[:, c] + dot(g, prefix, 1, 1)).astype(BF16)
        kg_ref[:, c] = (acc_k[:, c] + dot(v, suffix, 1, 1)).astype(BF16)
        vg_ref[:, c] = (acc_v[:, c] + dot(k, suffix, 1, 0)).astype(BF16)

    for h in range(first, heads):
        y_copy(h).wait_recv()
        give(h, z_in[h] + y_in[h])
        if h - first < first:
            finish(h - first)

    for h in range(first, heads):
        finish(h)

    for h in range(heads):
        sib_copy(h).wait_send()
        y_copy(h).wait_send()
        ret_copy(h).wait_send()

        @pl.when(has_next)
        def _():
            z_copy(h).wait_send()


def store_kernel(a_in, q_in, k_in, v_in, a_out, q_out, k_out, v_out, sems):
    pairs = ((a_in, a_out), (q_in, q_out), (k_in, k_out), (v_in, v_out))
    copies = [
        pltpu.make_async_copy(src, dst, sems.at[i]) for i, (src, dst) in enumerate(pairs)
    ]
    for copy in copies:
        copy.start()
    for copy in copies:
        copy.wait()


def body(planes, query_rows, key_rows, value_rows, out_grad):
    tokens, width = query_rows.shape
    heads = width // DH
    out = jax.ShapeDtypeStruct((tokens, width), BF16)
    mat = pltpu.VMEM((heads, DH, DH), F32)
    mat2 = pltpu.VMEM((2, heads, DH, DH), F32)
    rows16 = pltpu.VMEM((tokens, width), BF16)
    rows32 = pltpu.VMEM((tokens, width), F32)
    sem = pltpu.SemaphoreType.DMA((heads,))
    results = pl.pallas_call(
        functools.partial(kernel, planes, heads),
        out_shape=[out] * 4,
        in_specs=[pl.BlockSpec(memory_space=pltpu.HBM)] * 4,
        out_specs=[pl.BlockSpec(memory_space=pltpu.VMEM)] * 4,
        scratch_shapes=[rows16] * 5
        + [mat2, mat, mat, mat, mat, mat, mat, mat2]
        + [rows32] * 4
        + [pltpu.SemaphoreType.DMA((4, heads))]
        + [sem] * 8,
        compiler_params=pltpu.CompilerParams(
            collective_id=0, has_side_effects=True, vmem_limit_bytes=40 * 1024 * 1024
        ),
        cost_estimate=pl.CostEstimate(
            flops=18 * tokens * tokens * width, bytes_accessed=16 * tokens * width, transcendentals=0
        ),
    )(*(pltpu.with_memory_space_constraint(x, pltpu.HBM) for x in (query_rows, key_rows, value_rows, out_grad)))
    return pl.pallas_call(
        store_kernel,
        out_shape=[out] * 4,
        in_specs=[pl.BlockSpec(memory_space=pltpu.VMEM)] * 4,
        out_specs=[pl.BlockSpec(memory_space=pltpu.HBM)] * 4,
        scratch_shapes=[pltpu.SemaphoreType.DMA((4,))],
        compiler_params=pltpu.CompilerParams(vmem_limit_bytes=123 * 1024 * 1024 // 2),
    )(*(pltpu.with_memory_space_constraint(x, pltpu.VMEM) for x in results))


def solution(mesh):
    spec = P(("groups", "ctx"), None)
    return jax.shard_map(
        functools.partial(body, mesh.shape["ctx"] // 4),
        mesh=mesh,
        in_specs=(spec,) * 4,
        out_specs=(spec,) * 4,
        check_vma=False,
    )
```

```python
import functools

import jax
import jax.numpy as jnp
from jax import lax
from jax.experimental import pallas as pl
from jax.experimental.pallas import tpu as pltpu
from jax.sharding import PartitionSpec as P

DH = 128
MESH = pl.DeviceIdType.MESH
F32 = jnp.float32
BF16 = jnp.bfloat16


def dot(a, b, ca, cb):
    return lax.dot_general(a, b, (((ca,), (cb,)), ((), ())), preferred_element_type=F32)


def kernel(
    planes,
    heads,
    q_hbm,
    k_hbm,
    v_hbm,
    do_hbm,
    att_ref,
    qg_ref,
    kg_ref,
    vg_ref,
    q_ref,
    k_ref,
    v_ref,
    do_ref,
    g_ref,
    state,
    sib_in,
    y_out,
    y_in,
    z_out,
    z_in,
    ret_out,
    total,
    acc_a,
    acc_q,
    acc_k,
    acc_v,
    load_sem,
    sib_s,
    sib_r,
    y_s,
    y_r,
    z_s,
    z_r,
    ret_s,
    ret_r,
):
    tokens = q_ref.shape[0]
    group = lax.axis_index("groups")
    me = lax.axis_index("ctx")
    core = lax.rem(me, 2)
    row = lax.rem(me // 2, 2)
    plane = me // 4
    other = 1 - core
    step = 4 * (1 - 2 * core)
    has_prev = jnp.where(core == 0, plane > 0, plane < planes - 1)
    has_next = jnp.where(core == 0, plane < planes - 1, plane > 0)
    sibling = me + 1 - 2 * core
    partner = me + 2 - 4 * row
    is_low = row == core
    low = jnp.where(is_low, 1.0, 0.0).astype(F32)
    high = 1.0 - low

    def cols(h):
        return pl.ds(h * DH, DH)

    barrier = pltpu.get_barrier_semaphore()
    for device in (sibling, partner):
        pl.semaphore_signal(barrier, inc=1, device_id=(group, device), device_id_type=MESH)

    @pl.when(has_prev)
    def _():
        pl.semaphore_signal(barrier, inc=1, device_id=(group, me - step), device_id_type=MESH)

    @pl.when(has_next)
    def _():
        pl.semaphore_signal(barrier, inc=1, device_id=(group, me + step), device_id_type=MESH)

    first = 3 * heads // 8
    order = [h for i in range(heads) for h in (i, first + i) if i < first or h >= first]
    order = [h for n, h in enumerate(order) if h < heads and h not in order[:n]]

    last = heads - first
    early = [[h] if h < first // 2 else [] for h in range(last)]
    rest = []
    for n in range(max(first, last)):
        rest += [first + n] if n < last else []
        rest += [first // 2 + n] if first // 2 + n < first else []
    y_send = [(has_next if h < first else has_prev) | is_low for h in range(heads)]
    y_recv = [(has_next if h < first else has_prev) | jnp.logical_not(is_low) for h in range(heads)]

    loads = {}
    for h in order:
        for i, (src, dst) in enumerate(
            ((q_hbm, q_ref), (k_hbm, k_ref), (v_hbm, v_ref), (do_hbm, do_ref))
        ):
            loads[h, i] = pltpu.make_async_copy(
                src.at[:, cols(h)], dst.at[:, cols(h)], load_sem.at[i, h]
            )
            loads[h, i].start()

    @pl.when(jnp.logical_not(has_prev))
    def _():
        z_in[...] = jnp.zeros_like(z_in)

    for h in (0, first):
        @pl.when(jnp.logical_not(y_recv[h]))
        def _():
            size = first if h == 0 else heads - first
            y_in[pl.ds(h, size)] = jnp.zeros((size, DH, DH), F32)

    def remote(src, dst, send, recv, device):
        return pltpu.make_async_remote_copy(
            src_ref=src,
            dst_ref=dst,
            send_sem=send,
            recv_sem=recv,
            device_id=(group, device),
            device_id_type=MESH,
        )

    def sib_copy(h):
        return remote(state.at[other, h], sib_in.at[h], sib_s.at[h], sib_r.at[h], sibling)

    def y_copy(h):
        return remote(y_out.at[h], y_in.at[h], y_s.at[h], y_r.at[h], partner)

    def z_copy(h):
        return remote(z_out.at[h], z_in.at[h], z_s.at[h], z_r.at[h], me + step)

    def ret_copy(h):
        return remote(ret_out.at[h], total.at[core, h], ret_s.at[h], ret_r.at[h], sibling)

    position = (me * tokens + lax.broadcasted_iota(jnp.int32, (tokens, DH), 0)).astype(F32)
    scale = 1.0 / jnp.sqrt(DH * (position + 1.0))

    def wait_plane(h):
        @pl.when(has_prev)
        def _():
            z_copy(h).wait_recv()

    def send_plane(h):
        @pl.when(has_next)
        def _():
            z_copy(h).start()

    def cross(h):
        @pl.when(y_send[h])
        def _():
            y_copy(h).start()

    def pass_on(h):
        wait_plane(h)
        here = state[core, h] + sib_in[h]
        z_out[h] = z_in[h] + here
        send_plane(h)
        y_out[h] = z_in[h] + low * here
        cross(h)

    def chip_sum(h):
        sib_copy(h).wait_recv()
        if h < first:
            y_out[h] = state[core, h] + sib_in[h]
            cross(h)
        else:
            pl.when(jnp.logical_not(has_prev))(functools.partial(pass_on, h))

    for n, h in enumerate(order):
        for i in range(4):
            loads[h, i].wait()
        g = (scale * do_ref[:, cols(h)].astype(F32)).astype(BF16)
        g_ref[:, cols(h)] = g
        state[0, h] = dot(k_ref[:, cols(h)], v_ref[:, cols(h)], 0, 0)
        state[1, h] = dot(q_ref[:, cols(h)], g, 0, 0)
        if n == 0:
            pl.semaphore_wait(
                barrier, 2 + has_prev.astype(jnp.int32) + has_next.astype(jnp.int32)
            )
        sib_copy(h).start()
        if n >= 4:
            chip_sum(order[n - 4])
    for h in order[max(heads - 4, 0) :]:
        chip_sum(h)

    def local(h):
        c = cols(h)
        q, k, v, g = q_ref[:, c], k_ref[:, c], v_ref[:, c], g_ref[:, c]
        t = lax.broadcasted_iota(jnp.int32, (tokens, tokens), 0)
        s = lax.broadcasted_iota(jnp.int32, (tokens, tokens), 1)
        scores = jnp.where(t >= s, dot(q, k, 1, 1), 0.0).astype(BF16)
        dscores = jnp.where(t >= s, dot(g, v, 1, 1), 0.0).astype(BF16)
        acc_a[:, c] = dot(scores, v, 1, 0)
        acc_q[:, c] = dot(dscores, k, 1, 0)
        acc_k[:, c] = dot(dscores, q, 0, 0)
        acc_v[:, c] = dot(scores, g, 0, 0)

    def give(h, base):
        total[core, h] = base
        ret_out[h] = base + state[core, h]
        ret_copy(h).start()

    for h in range(first, heads):
        pl.when(has_prev)(functools.partial(pass_on, h))
        local(h)

    for h in range(first):
        @pl.when(y_recv[h])
        def _():
            y_copy(h).wait_recv()

        wait_plane(h)
        before = z_in[h]
        crossed = y_in[h]

        @pl.when(has_next)
        def _():
            z_out[h] = before + (state[core, h] + sib_in[h] + crossed)
            z_copy(h).start()

        give(h, before + high * crossed)
        local(h)

    def finish(h):
        ret_copy(h).wait_recv()
        c = cols(h)
        q, k, v, g = q_ref[:, c], k_ref[:, c], v_ref[:, c], g_ref[:, c]
        prefix = total[0, h].astype(BF16)
        suffix = total[1, h].astype(BF16)
        att_ref[:, c] = (scale * (acc_a[:, c] + dot(q, prefix, 1, 0))).astype(BF16)
        qg_ref[:, c] = (acc_q[:, c] + dot(g, prefix, 1, 1)).astype(BF16)
        kg_ref[:, c] = (acc_k[:, c] + dot(v, suffix, 1, 1)).astype(BF16)
        vg_ref[:, c] = (acc_v[:, c] + dot(k, suffix, 1, 0)).astype(BF16)

    for n, h in enumerate(range(first, heads)):
        @pl.when(y_recv[h])
        def _():
            y_copy(h).wait_recv()

        give(h, z_in[h] + y_in[h])
        for done in early[n]:
            finish(done)

    for h in rest:
        finish(h)

    for h in range(heads):
        sib_copy(h).wait_send()
        ret_copy(h).wait_send()

        @pl.when(y_send[h])
        def _():
            y_copy(h).wait_send()

        @pl.when(has_next)
        def _():
            z_copy(h).wait_send()


def store_kernel(a_in, q_in, k_in, v_in, a_out, q_out, k_out, v_out, sems):
    pairs = ((a_in, a_out), (q_in, q_out), (k_in, k_out), (v_in, v_out))
    copies = [
        pltpu.make_async_copy(src, dst, sems.at[i]) for i, (src, dst) in enumerate(pairs)
    ]
    for copy in copies:
        copy.start()
    for copy in copies:
        copy.wait()


def body(planes, query_rows, key_rows, value_rows, out_grad):
    tokens, width = query_rows.shape
    heads = width // DH
    out = jax.ShapeDtypeStruct((tokens, width), BF16)
    mat = pltpu.VMEM((heads, DH, DH), F32)
    mat2 = pltpu.VMEM((2, heads, DH, DH), F32)
    rows16 = pltpu.VMEM((tokens, width), BF16)
    rows32 = pltpu.VMEM((tokens, width), F32)
    sem = pltpu.SemaphoreType.DMA((heads,))
    results = pl.pallas_call(
        functools.partial(kernel, planes, heads),
        out_shape=[out] * 4,
        in_specs=[pl.BlockSpec(memory_space=pltpu.HBM)] * 4,
        out_specs=[pl.BlockSpec(memory_space=pltpu.VMEM)] * 4,
        scratch_shapes=[rows16] * 5
        + [mat2, mat, mat, mat, mat, mat, mat, mat2]
        + [rows32] * 4
        + [pltpu.SemaphoreType.DMA((4, heads))]
        + [sem] * 8,
        compiler_params=pltpu.CompilerParams(
            collective_id=0, has_side_effects=True, vmem_limit_bytes=40 * 1024 * 1024
        ),
        cost_estimate=pl.CostEstimate(
            flops=18 * tokens * tokens * width, bytes_accessed=16 * tokens * width, transcendentals=0
        ),
    )(*(pltpu.with_memory_space_constraint(x, pltpu.HBM) for x in (query_rows, key_rows, value_rows, out_grad)))
    return pl.pallas_call(
        store_kernel,
        out_shape=[out] * 4,
        in_specs=[pl.BlockSpec(memory_space=pltpu.VMEM)] * 4,
        out_specs=[pl.BlockSpec(memory_space=pltpu.HBM)] * 4,
        scratch_shapes=[pltpu.SemaphoreType.DMA((4,))],
        compiler_params=pltpu.CompilerParams(vmem_limit_bytes=123 * 1024 * 1024 // 2),
    )(*(pltpu.with_memory_space_constraint(x, pltpu.VMEM) for x in results))


def solution(mesh):
    spec = P(("groups", "ctx"), None)
    return jax.shard_map(
        functools.partial(body, mesh.shape["ctx"] // 4),
        mesh=mesh,
        in_specs=(spec,) * 4,
        out_specs=(spec,) * 4,
        check_vma=False,
    )
```

```python
import functools

import jax
import jax.numpy as jnp
from jax import lax
from jax.experimental import pallas as pl
from jax.experimental.pallas import tpu as pltpu
from jax.sharding import PartitionSpec as P

DH = 128
MESH = pl.DeviceIdType.MESH
F32 = jnp.float32
BF16 = jnp.bfloat16


def dot(a, b, ca, cb):
    return lax.dot_general(a, b, (((ca,), (cb,)), ((), ())), preferred_element_type=F32)


def kernel(
    planes,
    heads,
    q_hbm,
    k_hbm,
    v_hbm,
    do_hbm,
    att_ref,
    qg_ref,
    kg_ref,
    vg_ref,
    q_ref,
    k_ref,
    v_ref,
    do_ref,
    g_ref,
    state,
    sib_in,
    y_out,
    y_in,
    z_out,
    z_in,
    ret_out,
    total,
    acc_a,
    acc_q,
    acc_k,
    acc_v,
    load_sem,
    sib_s,
    sib_r,
    y_s,
    y_r,
    z_s,
    z_r,
    ret_s,
    ret_r,
):
    tokens = q_ref.shape[0]
    group = lax.axis_index("groups")
    me = lax.axis_index("ctx")
    core = lax.rem(me, 2)
    row = lax.rem(me // 2, 2)
    plane = me // 4
    other = 1 - core
    step = 4 * (1 - 2 * core)
    has_prev = jnp.where(core == 0, plane > 0, plane < planes - 1)
    has_next = jnp.where(core == 0, plane < planes - 1, plane > 0)
    sibling = me + 1 - 2 * core
    partner = me + 2 - 4 * row
    is_low = row == core
    low = jnp.where(is_low, 1.0, 0.0).astype(F32)
    high = 1.0 - low

    def cols(h):
        return pl.ds(h * DH, DH)

    barrier = pltpu.get_barrier_semaphore()
    for device in (sibling, partner):
        pl.semaphore_signal(barrier, inc=1, device_id=(group, device), device_id_type=MESH)

    @pl.when(has_prev)
    def _():
        pl.semaphore_signal(barrier, inc=1, device_id=(group, me - step), device_id_type=MESH)

    @pl.when(has_next)
    def _():
        pl.semaphore_signal(barrier, inc=1, device_id=(group, me + step), device_id_type=MESH)

    first = heads // 4
    order = [h for i in range(heads) for h in (i, first + i) if i < first or h >= first]
    order = [h for n, h in enumerate(order) if h < heads and h not in order[:n]]

    last = heads - first
    early = [[h] if h < first // 2 else [] for h in range(last)]
    rest = []
    for n in range(max(first, last)):
        rest += [first + n] if n < last else []
        rest += [first // 2 + n] if first // 2 + n < first else []
    y_send = [(has_next if h < first else has_prev) | is_low for h in range(heads)]
    y_recv = [(has_next if h < first else has_prev) | jnp.logical_not(is_low) for h in range(heads)]

    loads = {}
    for h in order:
        for i, (src, dst) in enumerate(
            ((q_hbm, q_ref), (k_hbm, k_ref), (v_hbm, v_ref), (do_hbm, do_ref))
        ):
            loads[h, i] = pltpu.make_async_copy(
                src.at[:, cols(h)], dst.at[:, cols(h)], load_sem.at[i, h]
            )
            loads[h, i].start()

    @pl.when(jnp.logical_not(has_prev))
    def _():
        z_in[...] = jnp.zeros_like(z_in)

    for h in (0, first):
        @pl.when(jnp.logical_not(y_recv[h]))
        def _():
            size = first if h == 0 else heads - first
            y_in[pl.ds(h, size)] = jnp.zeros((size, DH, DH), F32)

    def remote(src, dst, send, recv, device):
        return pltpu.make_async_remote_copy(
            src_ref=src,
            dst_ref=dst,
            send_sem=send,
            recv_sem=recv,
            device_id=(group, device),
            device_id_type=MESH,
        )

    def sib_copy(h):
        return remote(state.at[other, h], sib_in.at[h], sib_s.at[h], sib_r.at[h], sibling)

    def y_copy(h):
        return remote(y_out.at[h], y_in.at[h], y_s.at[h], y_r.at[h], partner)

    def z_copy(h):
        return remote(z_out.at[h], z_in.at[h], z_s.at[h], z_r.at[h], me + step)

    def ret_copy(h):
        return remote(ret_out.at[h], total.at[core, h], ret_s.at[h], ret_r.at[h], sibling)

    position = (me * tokens + lax.broadcasted_iota(jnp.int32, (tokens, DH), 0)).astype(F32)
    scale = 1.0 / jnp.sqrt(DH * (position + 1.0))

    def wait_plane(h):
        @pl.when(has_prev)
        def _():
            z_copy(h).wait_recv()

    def send_plane(h):
        @pl.when(has_next)
        def _():
            z_copy(h).start()

    def cross(h):
        @pl.when(y_send[h])
        def _():
            y_copy(h).start()

    def pass_on(h):
        wait_plane(h)
        here = state[core, h] + sib_in[h]
        z_out[h] = z_in[h] + here
        send_plane(h)
        y_out[h] = z_in[h] + low * here
        cross(h)

    def chip_sum(h):
        sib_copy(h).wait_recv()
        if h < first:
            y_out[h] = state[core, h] + sib_in[h]
            cross(h)
        else:
            pl.when(jnp.logical_not(has_prev))(functools.partial(pass_on, h))

    for n, h in enumerate(order):
        for i in range(4):
            loads[h, i].wait()
        g = (scale * do_ref[:, cols(h)].astype(F32)).astype(BF16)
        g_ref[:, cols(h)] = g
        state[0, h] = dot(k_ref[:, cols(h)], v_ref[:, cols(h)], 0, 0)
        state[1, h] = dot(q_ref[:, cols(h)], g, 0, 0)
        if n == 0:
            pl.semaphore_wait(
                barrier, 2 + has_prev.astype(jnp.int32) + has_next.astype(jnp.int32)
            )
        sib_copy(h).start()
        if n >= 4:
            chip_sum(order[n - 4])
    for h in order[max(heads - 4, 0) :]:
        chip_sum(h)

    def local(h):
        c = cols(h)
        q, k, v, g = q_ref[:, c], k_ref[:, c], v_ref[:, c], g_ref[:, c]
        t = lax.broadcasted_iota(jnp.int32, (tokens, tokens), 0)
        s = lax.broadcasted_iota(jnp.int32, (tokens, tokens), 1)
        scores = jnp.where(t >= s, dot(q, k, 1, 1), 0.0).astype(BF16)
        dscores = jnp.where(t >= s, dot(g, v, 1, 1), 0.0).astype(BF16)
        acc_a[:, c] = dot(scores, v, 1, 0)
        acc_q[:, c] = dot(dscores, k, 1, 0)
        acc_k[:, c] = dot(dscores, q, 0, 0)
        acc_v[:, c] = dot(scores, g, 0, 0)

    def give(h, base):
        total[core, h] = base
        ret_out[h] = base + state[core, h]
        ret_copy(h).start()

    for h in range(first, heads):
        pl.when(has_prev)(functools.partial(pass_on, h))
        local(h)

    for h in range(first):
        @pl.when(y_recv[h])
        def _():
            y_copy(h).wait_recv()

        wait_plane(h)
        before = z_in[h]
        crossed = y_in[h]

        @pl.when(has_next)
        def _():
            z_out[h] = before + (state[core, h] + sib_in[h] + crossed)
            z_copy(h).start()

        give(h, before + high * crossed)
        local(h)

    def finish(h):
        ret_copy(h).wait_recv()
        c = cols(h)
        q, k, v, g = q_ref[:, c], k_ref[:, c], v_ref[:, c], g_ref[:, c]
        prefix = total[0, h].astype(BF16)
        suffix = total[1, h].astype(BF16)
        att_ref[:, c] = (scale * (acc_a[:, c] + dot(q, prefix, 1, 0))).astype(BF16)
        qg_ref[:, c] = (acc_q[:, c] + dot(g, prefix, 1, 1)).astype(BF16)
        kg_ref[:, c] = (acc_k[:, c] + dot(v, suffix, 1, 1)).astype(BF16)
        vg_ref[:, c] = (acc_v[:, c] + dot(k, suffix, 1, 0)).astype(BF16)

    for n, h in enumerate(range(first, heads)):
        @pl.when(y_recv[h])
        def _():
            y_copy(h).wait_recv()

        give(h, z_in[h] + y_in[h])
        for done in early[n]:
            finish(done)

    for h in rest:
        finish(h)

    for h in range(heads):
        sib_copy(h).wait_send()
        ret_copy(h).wait_send()

        @pl.when(y_send[h])
        def _():
            y_copy(h).wait_send()

        @pl.when(has_next)
        def _():
            z_copy(h).wait_send()


def store_kernel(a_in, q_in, k_in, v_in, a_out, q_out, k_out, v_out, sems):
    pairs = ((a_in, a_out), (q_in, q_out), (k_in, k_out), (v_in, v_out))
    copies = [
        pltpu.make_async_copy(src, dst, sems.at[i]) for i, (src, dst) in enumerate(pairs)
    ]
    for copy in copies:
        copy.start()
    for copy in copies:
        copy.wait()


def body(planes, query_rows, key_rows, value_rows, out_grad):
    tokens, width = query_rows.shape
    heads = width // DH
    out = jax.ShapeDtypeStruct((tokens, width), BF16)
    mat = pltpu.VMEM((heads, DH, DH), F32)
    mat2 = pltpu.VMEM((2, heads, DH, DH), F32)
    rows16 = pltpu.VMEM((tokens, width), BF16)
    rows32 = pltpu.VMEM((tokens, width), F32)
    sem = pltpu.SemaphoreType.DMA((heads,))
    results = pl.pallas_call(
        functools.partial(kernel, planes, heads),
        out_shape=[out] * 4,
        in_specs=[pl.BlockSpec(memory_space=pltpu.HBM)] * 4,
        out_specs=[pl.BlockSpec(memory_space=pltpu.VMEM)] * 4,
        scratch_shapes=[rows16] * 5
        + [mat2, mat, mat, mat, mat, mat, mat, mat2]
        + [rows32] * 4
        + [pltpu.SemaphoreType.DMA((4, heads))]
        + [sem] * 8,
        compiler_params=pltpu.CompilerParams(
            collective_id=0, has_side_effects=True, vmem_limit_bytes=40 * 1024 * 1024
        ),
        cost_estimate=pl.CostEstimate(
            flops=18 * tokens * tokens * width, bytes_accessed=16 * tokens * width, transcendentals=0
        ),
    )(*(pltpu.with_memory_space_constraint(x, pltpu.HBM) for x in (query_rows, key_rows, value_rows, out_grad)))
    return pl.pallas_call(
        store_kernel,
        out_shape=[out] * 4,
        in_specs=[pl.BlockSpec(memory_space=pltpu.VMEM)] * 4,
        out_specs=[pl.BlockSpec(memory_space=pltpu.HBM)] * 4,
        scratch_shapes=[pltpu.SemaphoreType.DMA((4,))],
        compiler_params=pltpu.CompilerParams(vmem_limit_bytes=123 * 1024 * 1024 // 2),
    )(*(pltpu.with_memory_space_constraint(x, pltpu.VMEM) for x in results))


def solution(mesh):
    spec = P(("groups", "ctx"), None)
    return jax.shard_map(
        functools.partial(body, mesh.shape["ctx"] // 4),
        mesh=mesh,
        in_specs=(spec,) * 4,
        out_specs=(spec,) * 4,
        check_vma=False,
    )
```
